32 devices in a mesh: batch: 4 (over y, core), seq: 8 (over z, x).
Axes of the slice: x: 2, y: 2, z: 4, core: 2. Of those that a mesh axis runs over, the one named last changes fastest.
Arguments:
- hidden_in: bfloat16 [32, 1024, 1024], P('batch', 'seq'), may hold values from -6 to 6
- cotangent: bfloat16 [32, 1024, 1024], P('batch', 'seq'), may hold values from -6 to 6
- lengths: int32 [32], P('batch'), may hold values from 128 to 1024, as said below
- ln1_gain: float32 [1024], replicated, may hold values from 0.7 to 1.3
- ln1_bias: float32 [1024], replicated, may hold values from -0.4 to 0.4
- ln2_gain: float32 [1024], replicated, may hold values from 0.7 to 1.3
- ln2_bias: float32 [1024], replicated, may hold values from -0.4 to 0.4
- qkv_weight: bfloat16 [1024, 3072], replicated, may hold values from -0.1875 to 0.1875
- qkv_bias: float32 [3072], replicated, may hold values from -3 to 3
- dense_weight: bfloat16 [1024, 1024], replicated, may hold values from -1.5 to 1.5
- dense_bias: float32 [1024], replicated, may hold values from -3 to 3
- up_weight: bfloat16 [1024, 4096], replicated, may hold values from -0.1875 to 0.1875
- up_bias: float32 [4096], replicated, may hold values from -3 to 3
- down_weight: bfloat16 [4096, 1024], replicated, may hold values from -0.09375 to 0.09375
- down_bias: float32 [1024], replicated, may hold values from -3 to 3
- feature_gain: float32 [16, 64], replicated, may hold values from 0.5 to 2
- projection: float32 [64, 64], replicated, may hold values from -0.75 to 0.75
Outputs:
- activations: bfloat16 [32, 1024, 1024], P('batch', 'seq')
- input_grad: float32 [32, 1024, 1024], P('batch', 'seq')
- ln1_gain_grad: float32 [1024], P(('batch', 'seq'))
- ln1_bias_grad: float32 [1024], P(('batch', 'seq'))
- ln2_gain_grad: float32 [1024], P(('batch', 'seq'))
- ln2_bias_grad: float32 [1024], P(('batch', 'seq'))
- qkv_weight_grad: float32 [1024, 3072], P(('batch', 'seq'))
- query_key_bias_grad: float32 [2048], P(('batch', 'seq'))
- value_bias_grad: float32 [1024], P(('batch', 'seq'))
- dense_weight_grad: float32 [1024, 1024], P(('batch', 'seq'))
- dense_bias_grad: float32 [1024], P(('batch', 'seq'))
- up_weight_grad: float32 [1024, 4096], P(('batch', 'seq'))
- up_bias_grad: float32 [4096], P(('batch', 'seq'))
- down_weight_grad: float32 [4096, 1024], P(('batch', 'seq'))
- down_bias_grad: float32 [1024], P(('batch', 'seq'))
- feature_gain_grad: float32 [16, 64], replicated
- projection_grad: float32 [64, 64], replicated
The draws below stay inside these ranges and needn't reach their ends.
Inputs may be any that keep to these rules, and one draw needn't show every extreme that they name: `lengths`: in each aligned group of 8 slots (one index of batch), one slot, chosen by the seed, has length 1024.
All inputs are finite; a program needn't handle non-finite values.
Results may differ from the reference program's by a relative error of at most 0.0086.
Values sent between devices are 32-bit elements; how exact they have to be, the bound alone decides.
A program may use at most 384 MiB of HBM per device.

```python
import math
import jax
import jax.numpy as jnp
from jax import lax

D = 1024
H = 16
HEAD = 64
ROT = 16
FF = 4096
F = 64
BLOCK = 64
LEAST = 128
SLOTS_DEV = 8
SLOT = 1024
SLOTS = 32


def draw_lengths(key, part):
    key = jax.random.fold_in(key, 11)
    spread_key, pick_key = jax.random.split(key)
    spread = jax.random.randint(spread_key, (SLOTS,), 0, 32)
    shorter = jnp.maximum(LEAST, SLOT // (1 + spread))
    groups = SLOTS // SLOTS_DEV
    chosen = jax.random.randint(pick_key, (groups,), 0, SLOTS_DEV)
    full_slot = jnp.arange(SLOTS) % SLOTS_DEV == jnp.repeat(chosen, SLOTS_DEV)
    return jnp.where(full_slot, SLOT, shorter).astype(jnp.int32)


def norm_params(key, salt):
    key = jax.random.fold_in(key, salt)
    gain_key, shift_key, order_key = jax.random.split(key, 3)
    half = D // 2
    half_gain = jax.random.uniform(gain_key, (half,), jnp.float32, 0.7, 1.3)
    half_shift = jax.random.uniform(shift_key, (half,), jnp.float32, -0.4, 0.4)
    order = jax.random.permutation(order_key, jnp.arange(D).astype(jnp.int32))
    gain = jnp.concatenate([half_gain, half_gain])[order]
    shift = jnp.concatenate([half_shift, -half_shift])[order]
    return (gain.astype(jnp.float32), shift.astype(jnp.float32))


def draw_ln1_gain(key, part):
    shared = norm_params(key, 21)
    return shared[0]


def draw_ln1_bias(key, part):
    shared = norm_params(key, 21)
    return shared[1]


def draw_ln2_gain(key, part):
    shared = norm_params(key, 37)
    return shared[0]


def draw_ln2_bias(key, part):
    shared = norm_params(key, 37)
    return shared[1]


def steps_of(rng, extent, pieces, least, high):
    level = 1.0
    for axis_at, blocks in pieces:
        draws = jax.random.uniform(jax.random.fold_in(jax.random.fold_in(rng, 6), axis_at), (blocks,), jnp.float32, least / len(pieces), high / len(pieces))
        level = level * jnp.repeat(jnp.exp(draws), extent[axis_at] // blocks).reshape((-1,) + (1,) * (len(extent) - 1 - axis_at))
    return level


def centred(stream_key, shape, scale, limit, cuts=(), kind=jnp.bfloat16):
    factor_of = steps_of(stream_key, shape, cuts, -0.22, 0.18) if cuts else 1.0
    result = jax.random.normal(stream_key, shape, jnp.float32) * scale * factor_of
    return jnp.minimum(jnp.maximum(result, -limit), limit).astype(kind)


def setup_inputs(seed: int = 0) -> dict:
    keys = jax.random.split(jax.random.key(seed), 18)
    return {
        "hidden_in": centred(keys[0], (SLOTS, SLOT, D), 1.0, 6.0, ((0, 4), (1, 8))),
        "cotangent": centred(keys[1], (SLOTS, SLOT, D), 1.0, 6.0, ((0, 4), (1, 8))),
        "lengths": draw_lengths(jax.random.fold_in(keys[17], 71), 0),
        "ln1_gain": draw_ln1_gain(jax.random.fold_in(keys[17], 71), 0),
        "ln1_bias": draw_ln1_bias(jax.random.fold_in(keys[17], 71), 0),
        "ln2_gain": draw_ln2_gain(jax.random.fold_in(keys[17], 71), 0),
        "ln2_bias": draw_ln2_bias(jax.random.fold_in(keys[17], 71), 0),
        "qkv_weight": centred(keys[7], (D, 3 * D), D ** -0.5, 0.1875),
        "qkv_bias": centred(keys[8], (3 * D,), 0.2, 3.0, (), jnp.float32),
        "dense_weight": centred(keys[9], (D, D), 16 ** -0.5, 1.5),
        "dense_bias": centred(keys[10], (D,), 0.2, 3.0, (), jnp.float32),
        "up_weight": centred(keys[11], (D, FF), D ** -0.5, 0.1875),
        "up_bias": centred(keys[12], (FF,), 0.2, 3.0, (), jnp.float32),
        "down_weight": centred(keys[13], (FF, D), FF ** -0.5, 0.09375),
        "down_bias": centred(keys[14], (D,), 0.2, 3.0, (), jnp.float32),
        "feature_gain": jnp.clip(jnp.exp(jax.random.uniform(keys[15], (H, F), jnp.float32, math.log(0.5), math.log(2.0))), 0.5, 2.0),
        "projection": centred(keys[16], (HEAD, F), HEAD ** -0.5, 0.75, (), jnp.float32),
    }


HIGH = lax.Precision.HIGHEST

@jax.custom_vjp
def low(v):
    return lax.optimization_barrier(v.astype(jnp.bfloat16)).astype(jnp.float32)

@jax.custom_vjp
def low_back(v):
    return v

def low_keep(v):
    return (low(v), None)

def low_pass(kept, grad):
    return (grad,)

def back_keep(v):
    return (v, None)

def back_low(kept, grad):
    return (low(grad),)
low.defvjp(low_keep, low_pass)
low_back.defvjp(back_keep, back_low)

def matmul(left, right):
    return jnp.dot(left, right, precision=HIGH)

def layer_norm(values, gain, shift):
    center = values - lax.optimization_barrier(jnp.mean(values, axis=-1, keepdims=True))
    return center * lax.rsqrt(lax.optimization_barrier(jnp.mean(center * center, axis=-1, keepdims=True)) + 1e-05) * gain + shift

def dct_matrix(width):
    frequency = jnp.arange(width)[:, None].astype(jnp.float32)
    position = jnp.arange(width)[None, :].astype(jnp.float32)
    cosines = jnp.sqrt(2.0 / width) * jnp.cos(jnp.pi * (2.0 * position + 1.0) * frequency / (2.0 * width))
    return jnp.where(frequency == 0.0, cosines / jnp.sqrt(2.0), cosines)

def rotate(values, cosine, sine):
    half_rot = cosine.shape[-1]
    first_half = values[..., :half_rot]
    second_half = values[..., half_rot:2 * half_rot]
    remainder = values[..., 2 * half_rot:]
    return jnp.concatenate([first_half * cosine - second_half * sine, second_half * cosine + first_half * sine, remainder], axis=-1)

def features(values, feature_gain, projection, dct_rows):
    coeffs = jnp.einsum('phd,fd->phf', values, dct_rows, precision=HIGH)
    return feature_gain * jnp.exp(jnp.einsum('phf,fi->phi', coeffs, projection, precision=HIGH))

def attend(query_feat, key_feat, value_low):
    positions, heads, feats = query_feat.shape
    head_dim = value_low.shape[-1]
    block_count = positions // BLOCK
    query_blocks = query_feat.reshape(block_count, BLOCK, heads, feats)
    key_blocks = key_feat.reshape(block_count, BLOCK, heads, feats)
    value_blocks = value_low.reshape(block_count, BLOCK, heads, head_dim)
    causal = (jnp.arange(BLOCK)[:, None] >= jnp.arange(BLOCK)[None, :]).astype(jnp.float32)

    @jax.checkpoint
    def block_step(carried, blocks):
        key_state, norm_sum = carried
        query_block, key_block, value_block = blocks
        scores = jnp.einsum('phf,rhf->hpr', query_block, key_block, precision=HIGH) * causal
        numerator = jnp.einsum('hpr,rhe->phe', scores, value_block, precision=HIGH) + jnp.einsum('phf,hfe->phe', query_block, key_state, precision=HIGH)
        denominator = jnp.transpose(lax.optimization_barrier(jnp.sum(scores, axis=-1))) + jnp.einsum('phf,hf->ph', query_block, norm_sum, precision=HIGH)
        key_state = key_state + jnp.einsum('rhf,rhe->hfe', key_block, value_block, precision=HIGH)
        norm_sum = norm_sum + lax.optimization_barrier(jnp.sum(key_block, axis=0))
        return ((key_state, norm_sum), numerator / denominator[..., None])
    start = (jnp.zeros((heads, feats, head_dim), jnp.float32), jnp.zeros((heads, feats), jnp.float32))
    final_carry, outputs = lax.scan(block_step, start, (query_blocks, key_blocks, value_blocks))
    return outputs.reshape(positions, heads, head_dim)

def forward(hidden, ln1_gain, ln1_bias, ln2_gain, ln2_bias, qkv_weight, qkv_bias, dense_weight, dense_bias, up_weight, up_bias, down_weight, down_bias, feature_gain, projection, live_rows, cosine, sine):
    slot_len, width = hidden.shape
    heads = feature_gain.shape[0]
    head_dim = width // heads
    first_in = low(layer_norm(hidden, ln1_gain, ln1_bias))
    second_in = low(layer_norm(hidden, ln2_gain, ln2_bias))
    projected = low_back(matmul(first_in, qkv_weight) + qkv_bias)
    query_part = projected[:, :width].reshape(slot_len, heads, head_dim)
    key_part = projected[:, width:2 * width].reshape(slot_len, heads, head_dim)
    value_part = projected[:, 2 * width:].reshape(slot_len, heads, head_dim)
    dct_rows = dct_matrix(head_dim)
    query_feat = low(features(rotate(query_part, cosine, sine), feature_gain, projection, dct_rows))
    key_feat = low(features(rotate(key_part, cosine, sine), feature_gain, projection, dct_rows)) * live_rows[:, None, None]
    value_low = low(value_part)
    mixed = attend(query_feat, key_feat, value_low).reshape(slot_len, width)
    attn_low = low(low_back(mixed))
    attn_branch = matmul(attn_low, dense_weight) + dense_bias
    pre_act = low_back(matmul(second_in, up_weight) + up_bias)
    act_low = low(jax.nn.gelu(pre_act, approximate=False))
    return hidden + attn_branch + matmul(act_low, down_weight) + down_bias

def reference(hidden_in, cotangent, lengths, ln1_gain, ln1_bias, ln2_gain, ln2_bias, qkv_weight, qkv_bias, dense_weight, dense_bias, up_weight, up_bias, down_weight, down_bias, feature_gain, projection):
    slot_len = hidden_in.shape[1]
    width = hidden_in.shape[2]
    weights = tuple((weight_item.astype(jnp.float32) for weight_item in (ln1_gain, ln1_bias, ln2_gain, ln2_bias, qkv_weight, qkv_bias, dense_weight, dense_bias, up_weight, up_bias, down_weight, down_bias, feature_gain, projection)))
    half_rot = ROT // 2
    frequency = 10000.0 ** (-2.0 * jnp.arange(half_rot).astype(jnp.float32) / ROT)
    angle = jnp.arange(slot_len).astype(jnp.float32)[:, None] * frequency[None, :]
    cosine = jnp.cos(angle)[:, None, :]
    sine = jnp.sin(angle)[:, None, :]

    def per_slot(totals, slot_item):
        hidden_slot, grad_slot, length_slot = slot_item
        live_rows = (jnp.arange(slot_len).astype(jnp.int32) < length_slot).astype(jnp.float32)

        def apply_layer(hidden_value, *params):
            return forward(hidden_value, *params, live_rows, cosine, sine)
        output, pullback = jax.vjp(apply_layer, hidden_slot, *weights)
        grads = pullback(grad_slot)
        summed = tuple((total_item + grad_item for total_item, grad_item in zip(totals, grads[1:])))
        return (summed, (output.astype(jnp.bfloat16), grads[0]))
    start = tuple((jnp.zeros_like(weight_item) for weight_item in weights))
    totals, (outputs, input_grads) = lax.scan(per_slot, start, (hidden_in.astype(jnp.float32), cotangent.astype(jnp.float32), lengths))
    return (outputs, input_grads, totals[0], totals[1], totals[2], totals[3], totals[4], totals[5][:2 * width], totals[5][2 * width:], totals[6], totals[7], totals[8], totals[9], totals[10], totals[11], totals[12], totals[13])
```

```python
import functools

import jax
import jax.numpy as jnp
import numpy as np
from jax import lax
from jax.experimental import pallas as pl
from jax.experimental.pallas import tpu as pltpu
from jax.sharding import PartitionSpec as P

ROT = 16
EPSILON = 1e-05
LANES = 128
WIDE = 256
TILE = 256
F32 = jnp.float32
BF16 = jnp.bfloat16
MESH = pl.DeviceIdType.MESH
VMEM = pl.BlockSpec(memory_space=pltpu.VMEM)
ANY = pl.BlockSpec(memory_space=pl.ANY)
LIMIT = 60 * 1024 * 1024


def dot(left, right):
    return jnp.dot(left, right, preferred_element_type=F32)


def dot_nt(left, right):
    return lax.dot_general(left, right, (((1,), (1,)), ((), ())), preferred_element_type=F32)


def dot_tn(left, right):
    return lax.dot_general(left, right, (((0,), (0,)), ((), ())), preferred_element_type=F32)


def split(values):
    high = values.astype(BF16)
    return high, (values - high.astype(F32)).astype(BF16)


def same_head(width, head):
    rows = lax.broadcasted_iota(jnp.int32, (width, width), 0) // head
    cols = lax.broadcasted_iota(jnp.int32, (width, width), 1) // head
    return rows == cols


def compact(square, mask, head):
    kept = jnp.where(mask, square, 0.0)
    total = kept[:head]
    for part in range(1, square.shape[0] // head):
        total = total + kept[part * head : (part + 1) * head]
    return total


def normalize(values):
    center = values - jnp.mean(values, axis=-1, keepdims=True)
    spread = lax.rsqrt(jnp.mean(center * center, axis=-1, keepdims=True) + EPSILON)
    return center * spread, spread


def roll_lanes(values, by):
    return pltpu.roll(values, by % values.shape[1], 1)


def dct_matrix(width):
    frequency = jnp.arange(width)[:, None].astype(F32)
    position = jnp.arange(width)[None, :].astype(F32)
    cosines = jnp.sqrt(2.0 / width) * jnp.cos(
        jnp.pi * (2.0 * position + 1.0) * frequency / (2.0 * width)
    )
    return jnp.where(frequency == 0.0, cosines / jnp.sqrt(2.0), cosines)


def front_kernel(
    hidden, weight, bias, gain1, shift1, gain2, shift2, cosine, sine_a, sine_b, map_high, map_low,
    feature_gain, live, first, second, query, key, value, query_rot, key_rot, state, total,
    *, toks, head,
):
    unit, _ = normalize(hidden[...].astype(F32))
    first[...] = (unit * gain1[...] + shift1[...]).astype(BF16)
    second[...] = (unit * gain2[...] + shift2[...]).astype(BF16)
    width = hidden.shape[1]
    mask = same_head(WIDE, head)

    def group(j, carry):
        cols = pl.ds(pl.multiple_of(j * WIDE, WIDE), WIDE)
        for at, feats, rotated in ((0, query, query_rot), (1, key, key_rot)):
            wcols = pl.ds(pl.multiple_of(at * width + j * WIDE, WIDE), WIDE)
            raw = dot(first[...], weight[:, wcols]) + bias[:, wcols]
            turned = (
                raw * cosine[...]
                + roll_lanes(raw, -(ROT // 2)) * sine_a[...]
                + roll_lanes(raw, ROT // 2) * sine_b[...]
            )
            high, low = split(turned)
            power = dot(high, map_high[...]) + dot(low, map_high[...]) + dot(high, map_low[...])
            phi = (feature_gain[:, cols] * jnp.exp(power)).astype(BF16)
            if at == 1:
                phi = phi * live[...].astype(BF16)
            feats[:, cols] = phi
            rotated[:, cols] = high
        wcols = pl.ds(pl.multiple_of(2 * width + j * WIDE, WIDE), WIDE)
        value[:, cols] = (dot(first[...], weight[:, wcols]) + bias[:, wcols]).astype(BF16)
        for slot in range(hidden.shape[0] // toks):
            rows = pl.ds(slot * toks, toks)
            keys = key[rows, cols]
            state[slot, :, cols] = compact(dot_tn(keys, value[rows, cols]), mask, head)
            total[slot, :, cols] = jnp.sum(keys.astype(F32), axis=0, keepdims=True)
        return carry

    lax.fori_loop(0, width // WIDE, group, 0)


def front(hidden, weight, bias, gain1, shift1, gain2, shift2, tables, maps, feature_gain, live, slots, head):
    rows, width = hidden.shape
    toks = rows // slots
    per = TILE // toks
    tile = pl.BlockSpec((TILE, width), lambda i: (i, 0))
    once = lambda shape: pl.BlockSpec(shape, lambda i: (0,) * len(shape))
    low = jax.ShapeDtypeStruct((rows, width), BF16)
    return pl.pallas_call(
        functools.partial(front_kernel, toks=toks, head=head),
        grid=(rows // TILE,),
        in_specs=[tile, once(weight.shape), once(bias.shape)]
        + [once((1, width))] * 4
        + [once((TILE, WIDE))] * 3
        + [once((WIDE, WIDE))] * 2
        + [once((1, width)), pl.BlockSpec((TILE, 1), lambda i: (i, 0))],
        out_specs=[tile] * 7
        + [
            pl.BlockSpec((per, head, width), lambda i: (i, 0, 0)),
            pl.BlockSpec((per, 1, width), lambda i: (i, 0, 0)),
        ],
        out_shape=[low] * 7
        + [
            jax.ShapeDtypeStruct((slots, head, width), F32),
            jax.ShapeDtypeStruct((slots, 1, width), F32),
        ],
        compiler_params=pltpu.CompilerParams(vmem_limit_bytes=LIMIT),
        name="front",
    )(hidden, weight, bias, gain1, shift1, gain2, shift2, *tables, *maps, feature_gain, live)


def seq_peer(offset):
    count = lax.axis_size("seq")
    return (lax.axis_index("batch"), lax.rem(lax.axis_index("seq") + offset, count))


def gather_small(value, held, send_sem, recv_sem):
    count = lax.axis_size("seq")
    me = lax.axis_index("seq")
    copies = []
    for offset in range(1, count):
        copy = pltpu.make_async_remote_copy(
            src_ref=value, dst_ref=held.at[me], send_sem=send_sem.at[offset - 1],
            recv_sem=recv_sem.at[offset - 1], device_id=seq_peer(offset), device_id_type=MESH,
        )
        copy.start()
        copies.append(copy)
    return copies


def greet_seq():
    barrier = pltpu.get_barrier_semaphore()
    count = lax.axis_size("seq")
    for offset in range(1, count):
        pl.semaphore_signal(barrier, inc=1, device_id=seq_peer(offset), device_id_type=MESH)
    pl.semaphore_wait(barrier, count - 1)


def sum_small(held, later):
    me = lax.axis_index("seq")
    total = jnp.zeros(held.shape[1:], F32)
    for at in range(held.shape[0]):
        use = (at > me) if later else (at < me)
        total = total + jnp.where(use, held[at], 0.0)
    return total


def middle_kernel(
    grad, dense, query, key, total, d_num, inverse, prior, stat, grad_sum, d_mixed, held, send_sem, recv_sem,
    *, slots, head,
):
    rows, width = grad.shape
    toks = rows // slots
    held[lax.axis_index("seq")] = jnp.zeros(total.shape, F32)
    greet_seq()
    copies = gather_small(total, held, send_sem, recv_sem)

    def rows_of(i, carry):
        at = pl.ds(pl.multiple_of(i * TILE, TILE), TILE)
        d_mixed[at] = dot_nt(grad[at], dense[...]).astype(BF16)
        return carry + jnp.sum(grad[at].astype(F32), axis=0, keepdims=True)

    grad_sum[...] = lax.fori_loop(0, rows // TILE, rows_of, jnp.zeros((1, width), F32))
    for copy in copies:
        copy.wait()
    prior[...] = sum_small(held, False)
    mask = same_head(WIDE, head)
    ones = mask.astype(BF16)
    lower = (
        lax.broadcasted_iota(jnp.int32, (toks, toks), 0)
        >= lax.broadcasted_iota(jnp.int32, (toks, toks), 1)
    ).astype(BF16)

    def slot_of(i, carry):
        at = pl.ds(pl.multiple_of(i * toks, toks), toks)
        for j in range(width // WIDE):
            cols = pl.ds(j * WIDE, WIDE)
            sums = dot(lower, key[at, cols]) + prior[i, :, cols]
            queries = query[at, cols]
            high, low = split(queries.astype(F32) * sums)
            inv = 1.0 / (dot(high, ones) + dot(low, ones))
            inverse[at, cols] = inv
            grads = (d_mixed[at, cols].astype(F32) * inv).astype(BF16)
            d_num[at, cols] = grads
            stat[i, :, cols] = compact(dot_tn(queries, grads), mask, head)
        return carry

    lax.fori_loop(0, slots, slot_of, 0)


def middle(grad, dense, query, key, total, slots, head):
    rows, width = grad.shape
    seq = lax.axis_size("seq")
    return pl.pallas_call(
        functools.partial(middle_kernel, slots=slots, head=head),
        in_specs=[VMEM] * 5,
        out_specs=[VMEM] * 5,
        out_shape=[
            jax.ShapeDtypeStruct((rows, width), BF16),
            jax.ShapeDtypeStruct((rows, width), F32),
            jax.ShapeDtypeStruct((slots, 1, width), F32),
            jax.ShapeDtypeStruct((slots, head, width), F32),
            jax.ShapeDtypeStruct((1, width), F32),
        ],
        scratch_shapes=[
            pltpu.VMEM((rows, width), BF16),
            pltpu.VMEM((seq, slots, 1, width), F32),
            pltpu.SemaphoreType.DMA((seq - 1,)),
            pltpu.SemaphoreType.DMA((seq - 1,)),
        ],
        compiler_params=pltpu.CompilerParams(
            collective_id=1, has_side_effects=True, vmem_limit_bytes=LIMIT
        ),
        name="middle",
    )(grad, dense, query, key, total)


def mlp_kernel(
    second, grad, up, up_bias, down, act, d_pre, branch, d_second, bias_grad, *, step
):
    chunk = up.shape[1]
    part = pl.program_id(0)

    @pl.when(part == 0)
    def _():
        branch[...] = jnp.zeros_like(branch)
        d_second[...] = jnp.zeros_like(d_second)

    def rows_of(i, total):
        at = pl.ds(pl.multiple_of(i * step, step), step)
        pre = dot(second[at], up[...]) + up_bias[...]
        cdf = 0.5 * (1.0 + lax.erf(pre * 0.7071067811865476))
        density = jnp.exp(-0.5 * pre * pre) * 0.3989422804014327
        hot = (pre * cdf).astype(BF16)
        act[at] = hot
        branch[at] += dot(hot, down[...])
        slope = (dot_nt(grad[at], down[...]) * (cdf + pre * density)).astype(BF16)
        d_pre[at] = slope
        d_second[at] += dot_nt(slope, up[...])
        return total + jnp.sum(slope.astype(F32), axis=0, keepdims=True)

    bias_grad[...] = lax.fori_loop(0, second.shape[0] // step, rows_of, jnp.zeros((1, chunk), F32))


def mlp(second, grad, up, up_bias, down):
    rows, width = second.shape
    hidden = up.shape[1]
    chunk = 512
    whole = pl.BlockSpec((rows, width), lambda i: (0, 0))
    cols = pl.BlockSpec((rows, chunk), lambda i: (0, i))
    return pl.pallas_call(
        functools.partial(mlp_kernel, step=TILE),
        grid=(hidden // chunk,),
        in_specs=[
            whole,
            whole,
            pl.BlockSpec((width, chunk), lambda i: (0, i)),
            pl.BlockSpec((1, chunk), lambda i: (0, i)),
            pl.BlockSpec((chunk, width), lambda i: (i, 0)),
        ],
        out_specs=[cols, cols, whole, whole, pl.BlockSpec((1, chunk), lambda i: (0, i))],
        out_shape=[
            jax.ShapeDtypeStruct((rows, hidden), BF16),
            jax.ShapeDtypeStruct((rows, hidden), BF16),
            jax.ShapeDtypeStruct((rows, width), F32),
            jax.ShapeDtypeStruct((rows, width), F32),
            jax.ShapeDtypeStruct((1, hidden), F32),
        ],
        compiler_params=pltpu.CompilerParams(vmem_limit_bytes=LIMIT),
        name="mlp",
    )(second, grad, up, up_bias, down)


def attend_kernel(
    query, key, value, query_rot, d_num, inverse, before, after, prior, cosine, sine_a, sine_b, map_back,
    mixed, d_query_out, d_value_out, d_key_out, query_norm, gain_sum, map_sum, bias_sum, *, head,
):
    toks, width = query.shape

    @pl.when(pl.program_id(0) == 0)
    def _():
        gain_sum[...] = jnp.zeros_like(gain_sum)
        map_sum[...] = jnp.zeros_like(map_sum)
        bias_sum[...] = jnp.zeros_like(bias_sum)

    lane = lax.broadcasted_iota(jnp.int32, (toks, LANES), 1)
    left = lane < head
    both = same_head(LANES, head)
    causal_row = lax.broadcasted_iota(jnp.int32, (toks, 2 * toks), 0)
    causal_col = lax.broadcasted_iota(jnp.int32, (toks, 2 * toks), 1)
    causal = causal_row >= jnp.where(causal_col >= toks, causal_col - toks, causal_col)
    sel_row = lax.broadcasted_iota(jnp.int32, (LANES, 2 * toks), 0) < head
    sel_col = lax.broadcasted_iota(jnp.int32, (LANES, 2 * toks), 1) < toks
    spread = jnp.concatenate([(sel_row == sel_col).astype(BF16), both.astype(BF16)], axis=1)
    zero = jnp.zeros((toks, LANES), BF16)

    def double(values):
        return jnp.concatenate([jnp.where(left, values, zero), jnp.where(left, zero, values)], axis=0)

    def diagonal(values):
        return split(jnp.where(both, jnp.concatenate([values, values], axis=0), 0.0))

    def merge(values):
        return jnp.where(left, values[:toks], values[toks:])

    def pair(j, carry):
        cols = pl.ds(pl.multiple_of(j * LANES, LANES), LANES)
        q, k, v, dn = query[:, cols], key[:, cols], value[:, cols], d_num[:, cols]
        keys, values = double(k), double(v)
        prior_state, later_state = diagonal(before[0, :, cols]), diagonal(after[0, :, cols])
        scores = jnp.where(causal, dot_nt(q, keys), 0.0).astype(BF16)
        mix = (dot(scores, values) + dot(q, prior_state[0]) + dot(q, prior_state[1])) * inverse[:, cols]
        mixed[:, cols] = mix.astype(BF16)
        high, low = split(dn.astype(F32) * mix)
        minus = dot(high, spread) + dot(low, spread)
        d_den = -minus[:, 2 * toks :]
        mixing = jnp.where(causal, dot_nt(dn, values) - minus[:, : 2 * toks], 0.0).astype(BF16)
        d_query = dot(mixing, keys) + dot_nt(dn, prior_state[0]) + dot_nt(dn, prior_state[1]) + d_den * prior[0, :, cols]
        d_key_out[:, cols] = merge(dot_tn(mixing, q)) + dot_nt(v, later_state[0]) + dot_nt(v, later_state[1])
        d_value = (merge(dot_tn(scores, dn)) + dot(k, later_state[0]) + dot(k, later_state[1])).astype(BF16)
        d_value_out[:, cols] = d_value
        wide = q.astype(F32)
        query_norm[0, :, cols] = jnp.sum(wide * d_den, axis=0, keepdims=True)
        slope = d_query * wide
        gain_sum[:, cols] += jnp.sum(slope, axis=0, keepdims=True)
        slope = slope.astype(BF16)
        map_sum[...] += dot_tn(query_rot[:, cols], slope)
        turned = dot(slope, map_back[...])
        d_raw = (
            turned * cosine[...]
            - roll_lanes(turned, -(ROT // 2)) * sine_a[...]
            - roll_lanes(turned, ROT // 2) * sine_b[...]
        ).astype(BF16)
        d_query_out[:, cols] = d_raw
        bias_sum[0, :, cols] += jnp.sum(d_raw.astype(F32), axis=0, keepdims=True)
        bias_sum[1, :, cols] += jnp.sum(d_value.astype(F32), axis=0, keepdims=True)
        return carry

    lax.fori_loop(0, width // LANES, pair, 0)


def attend(query, key, value, query_rot, d_num, inverse, before, after, prior, tables, map_back, slots, head):
    rows, width = query.shape
    toks = rows // slots
    tile = pl.BlockSpec((toks, width), lambda i: (i, 0))
    state = pl.BlockSpec((1, head, width), lambda i: (i, 0, 0))
    small = pl.BlockSpec((1, 1, width), lambda i: (i, 0, 0))
    once = lambda shape: pl.BlockSpec(shape, lambda i: (0,) * len(shape))
    return pl.pallas_call(
        functools.partial(attend_kernel, head=head),
        grid=(slots,),
        in_specs=[tile] * 6 + [state, state, small] + [once((toks, LANES))] * 3 + [once((LANES, LANES))],
        out_specs=[tile] * 4 + [small, once((1, width)), once((LANES, LANES)), once((2, 1, width))],
        out_shape=[
            jax.ShapeDtypeStruct((rows, width), BF16),
            jax.ShapeDtypeStruct((rows, width), BF16),
            jax.ShapeDtypeStruct((rows, width), BF16),
            jax.ShapeDtypeStruct((rows, width), F32),
            jax.ShapeDtypeStruct((slots, 1, width), F32),
            jax.ShapeDtypeStruct((1, width), F32),
            jax.ShapeDtypeStruct((LANES, LANES), F32),
            jax.ShapeDtypeStruct((2, 1, width), F32),
        ],
        compiler_params=pltpu.CompilerParams(vmem_limit_bytes=LIMIT),
        name="attend",
    )(query, key, value, query_rot, d_num, inverse, before, after, prior, *tables, map_back)


def back_kernel(
    hidden, grad, mixed, branch, d_second, key, key_rot, d_key_part, d_query, d_value, query_norm,
    qkv_weight, dense_weight, dense_bias, down_bias, gain1, gain2, cosine, sine_a, sine_b, map_back,
    output, input_grad, d_key_out, norm_sums, gain_sum, map_sum, bias_sum,
    held, later, send_sem, recv_sem, *, slots, head,
):
    rows, width = hidden.shape
    toks = rows // slots
    per = TILE // toks
    held[lax.axis_index("seq")] = jnp.zeros(query_norm.shape, F32)
    greet_seq()
    copies = gather_small(query_norm, held, send_sem, recv_sem)
    norm_sums[...] = jnp.zeros_like(norm_sums)
    gain_sum[...] = jnp.zeros_like(gain_sum)
    map_sum[...] = jnp.zeros_like(map_sum)
    bias_sum[...] = jnp.zeros_like(bias_sum)

    def forward_of(i, carry):
        at = pl.ds(pl.multiple_of(i * TILE, TILE), TILE)
        output[at] = (
            hidden[at].astype(F32)
            + (dot(mixed[at], dense_weight[...]) + dense_bias[...])
            + (branch[at] + down_bias[...])
        ).astype(BF16)
        return carry

    lax.fori_loop(0, rows // TILE, forward_of, 0)
    for copy in copies:
        copy.wait()
    later[...] = sum_small(held, True)

    def rows_of(i, carry):
        at = pl.ds(pl.multiple_of(i * TILE, TILE), TILE)
        for j in range(width // LANES):
            cols = pl.ds(j * LANES, LANES)
            extra = jnp.concatenate(
                [
                    jnp.broadcast_to(later[i * per + slot, :, cols], (toks, LANES))
                    for slot in range(per)
                ],
                axis=0,
            )
            slope = (d_key_part[at, cols] + extra) * key[at, cols].astype(F32)
            gain_sum[:, cols] += jnp.sum(slope, axis=0, keepdims=True)
            slope = slope.astype(BF16)
            map_sum[...] += dot_tn(key_rot[at, cols], slope)
            turned = dot(slope, map_back[...])
            d_raw = (
                turned * cosine[...]
                - roll_lanes(turned, -(ROT // 2)) * sine_a[...]
                - roll_lanes(turned, ROT // 2) * sine_b[...]
            ).astype(BF16)
            d_key_out[at, cols] = d_raw
            bias_sum[:, cols] += jnp.sum(d_raw.astype(F32), axis=0, keepdims=True)
        d_first = (
            dot_nt(d_query[at], qkv_weight[:, pl.ds(0, width)])
            + dot_nt(d_key_out[at], qkv_weight[:, pl.ds(width, width)])
            + dot_nt(d_value[at], qkv_weight[:, pl.ds(2 * width, width)])
        )
        unit, spread = normalize(hidden[at].astype(F32))
        total = grad[at].astype(F32)
        for which, d_out, gain in ((0, d_first, gain1), (1, d_second[at], gain2)):
            scaled = d_out * gain[...]
            inner = (
                scaled
                - jnp.mean(scaled, axis=-1, keepdims=True)
                - unit * jnp.mean(scaled * unit, axis=-1, keepdims=True)
            )
            total = total + spread * inner
            norm_sums[2 * which] += jnp.sum(d_out * unit, axis=0, keepdims=True)
            norm_sums[2 * which + 1] += jnp.sum(d_out, axis=0, keepdims=True)
        input_grad[at] = total
        return carry

    lax.fori_loop(0, rows // TILE, rows_of, 0)


def back(arrays, tables, map_back, slots, head):
    hidden = arrays[0]
    rows, width = hidden.shape
    seq = lax.axis_size("seq")
    inputs = (*arrays, *tables, map_back)
    return pl.pallas_call(
        functools.partial(back_kernel, slots=slots, head=head),
        in_specs=[VMEM] * len(inputs),
        out_specs=[VMEM] * 7,
        out_shape=[
            jax.ShapeDtypeStruct((rows, width), BF16),
            jax.ShapeDtypeStruct((rows, width), F32),
            jax.ShapeDtypeStruct((rows, width), BF16),
            jax.ShapeDtypeStruct((4, 1, width), F32),
            jax.ShapeDtypeStruct((1, width), F32),
            jax.ShapeDtypeStruct((LANES, LANES), F32),
            jax.ShapeDtypeStruct((1, width), F32),
        ],
        scratch_shapes=[
            pltpu.VMEM((seq, slots, 1, width), F32),
            pltpu.VMEM((slots, 1, width), F32),
            pltpu.SemaphoreType.DMA((seq - 1,)),
            pltpu.SemaphoreType.DMA((seq - 1,)),
        ],
        compiler_params=pltpu.CompilerParams(
            collective_id=2, has_side_effects=True, vmem_limit_bytes=LIMIT
        ),
        name="back",
    )(*inputs)


def sizes():
    count = lax.axis_size("seq")
    return {"y": lax.axis_size("batch") // 2, "core": 2, "far": 4, "near": count // 4}


def places():
    size = sizes()
    batch, seq = lax.axis_index("batch"), lax.axis_index("seq")
    return {
        "y": batch // 2, "core": lax.rem(batch, 2),
        "far": seq // size["near"], "near": lax.rem(seq, size["near"]),
    }


def peer(axis, offset):
    size, place = sizes(), places()
    place[axis] = lax.rem(place[axis] + offset, size[axis])
    return (place["y"] * 2 + place["core"], place["far"] * size["near"] + place["near"])


def greet(axes):
    barrier = pltpu.get_barrier_semaphore()
    size = sizes()
    total = 0
    for axis in axes:
        for offset in range(1, size[axis]):
            pl.semaphore_signal(barrier, inc=1, device_id=peer(axis, offset), device_id_type=MESH)
            total += 1
    pl.semaphore_wait(barrier, total)


NEAR_FIRST = ("near", "y", "far")
Y_FIRST = ("y", "near", "far")
LAG = (3, 5, 7)
CORE_SLOTS, SUM_SLOTS, STAGE_SLOTS = 2, 8, 4


def reduce_kernel(
    act, second, mixed, first, grad, d_pre, d_query, d_key, d_value, small,
    down_out, up_out, dense_out, qkv_out, small_out,
    rhs, send_core, recv_core, sums, recv_a, recv_b, recv_z, small_recv,
    rhs_sem, core_send, core_recv, a_send, a_recv, b_send, b_recv, z_send, z_recv, small_send, small_got,
    core_free, a_free, b_free, z_free,
):
    size, place = sizes(), places()
    width = grad.shape[1]
    inner = size["far"] * size["near"]
    greet(("core", "near", "y", "far"))

    chunks = [("down", act, None, i * WIDE, down_out, i * WIDE) for i in range(width // WIDE)]
    chunks += [("wide", second, d_pre, i * width, up_out, i * width) for i in range(d_pre.shape[1] // width)]
    chunks += [("wide", mixed, grad, 0, dense_out, 0)]
    chunks += [("wide", first, d, 0, qkv_out, i * width) for i, d in enumerate((d_query, d_key, d_value))]
    count = len(chunks)
    orders = [NEAR_FIRST if t % 2 == 0 else Y_FIRST for t in range(count)]

    def fetched(t):
        return t < count and chunks[t][2] is not None and chunks[t][2] is not grad

    def fetch(t):
        _, _, right, column, _, _ = chunks[t]
        return pltpu.make_async_copy(
            right.at[:, pl.ds(column, width)], rhs.at[t % 2], rhs_sem.at[t % 2]
        )

    def produce(t, core, into):
        kind, left, right, column, _, _ = chunks[t]
        order = orders[t]

        def block(y, carry):
            span = inner * (left.shape[1] // (inner * size["y"] * 2))
            start = pl.multiple_of((y * 2 + core) * span, span)
            columns = left[:, pl.ds(start, span)]
            if kind == "down":
                result = dot_tn(columns, grad[:, pl.ds(column, WIDE)])
            elif right is grad:
                result = dot_tn(columns, grad[...])
            else:
                result = dot_tn(columns, rhs[t % 2])
            high = span // inner
            for k in range(inner):
                at = {"y": y, "far": k // size["near"], "near": k % size["near"]}
                unit = (at[order[0]] * size[order[1]] + at[order[1]]) * size[order[2]] + at[order[2]]
                piece = result[k * high : (k + 1) * high]
                if kind == "down":
                    into[unit] = piece
                else:
                    for part in range(width // WIDE):
                        into[unit, pl.ds(part * high, high)] = piece[:, part * WIDE : (part + 1) * WIDE]
            return carry

        lax.fori_loop(0, size["y"], block, 0)

    def copy(source, target, send, recv, axis, offset):
        return pltpu.make_async_remote_copy(
            src_ref=source, dst_ref=target, send_sem=send, recv_sem=recv,
            device_id=peer(axis, offset), device_id_type=MESH,
        )

    def core_copy(t):
        slot = t % CORE_SLOTS
        return copy(
            send_core.at[slot], recv_core.at[slot], core_send.at[slot], core_recv.at[slot], "core", 1
        )

    received = (recv_a, recv_b, recv_z)
    sends, gots, frees = (a_send, b_send, z_send), (a_recv, b_recv, z_recv), (a_free, b_free, z_free)

    def spans(t, stage):
        order = orders[t]
        base, length = 0, size["y"] * inner
        for axis in order[:stage]:
            length //= size[axis]
            base = base + place[axis] * length
        return base, length // size[order[stage]]

    def stage_copies(t, stage):
        axis = orders[t][stage]
        base, part = spans(t, stage)
        slot = t % STAGE_SLOTS
        copies = []
        for offset in range(1, size[axis]):
            there = lax.rem(place[axis] + offset, size[axis])
            copies.append(
                copy(
                    sums.at[t % SUM_SLOTS, pl.ds(base + there * part, part)],
                    received[stage].at[slot, pl.ds((offset - 1) * part, part)],
                    sends[stage].at[slot, offset - 1], gots[stage].at[slot, offset - 1], axis, offset,
                )
            )
        return copies

    def stage_start(t, stage):
        for i, one in enumerate(stage_copies(t, stage)):
            if t >= STAGE_SLOTS:
                pl.semaphore_wait(frees[stage].at[t % 2, i], 1)
            one.start()

    def stage_add(t, stage):
        axis = orders[t][stage]
        base, part = spans(t, stage)
        here = base + place[axis] * part
        slot = t % STAGE_SLOTS
        for one in stage_copies(t, stage):
            one.wait()

        def add(u, carry):
            value = sums[t % SUM_SLOTS, here + u]
            for offset in range(1, size[axis]):
                value = value + received[stage][slot, (offset - 1) * part + u]
            sums[t % SUM_SLOTS, here + u] = value
            return carry

        lax.fori_loop(0, part, add, 0)
        if t + STAGE_SLOTS < count:
            for offset in range(1, size[axis]):
                pl.semaphore_signal(
                    frees[stage].at[t % 2, offset - 1], inc=1,
                    device_id=peer(axis, size[axis] - offset), device_id_type=MESH,
                )
        return here

    small_axes = ("core", "near", "y", "far")

    def small_copies(stage):
        axis = small_axes[stage]
        return [
            copy(
                small_out, small_recv.at[stage, offset - 1], small_send.at[stage, offset - 1],
                small_got.at[stage, offset - 1], axis, offset,
            )
            for offset in range(1, size[axis])
        ]

    small_out[...] = small[...]
    for one in small_copies(0):
        one.start()
    for t in range(2):
        if fetched(t):
            fetch(t).start()

    for t in range(count + LAG[2]):
        if 0 <= t - 1 < count:
            old = t - 1
            core_copy(old).wait_recv()

            def add_core(u, carry, old=old):
                sums[old % SUM_SLOTS, u] += recv_core[old % CORE_SLOTS, u]
                return carry

            lax.fori_loop(0, size["y"] * inner, add_core, 0)
            if old + CORE_SLOTS < count:
                pl.semaphore_signal(core_free, inc=1, device_id=peer("core", 1), device_id_type=MESH)
            stage_start(old, 0)
        if t < count:
            if fetched(t):
                fetch(t).wait()
            if t >= CORE_SLOTS:
                core_copy(t - CORE_SLOTS).wait_send()
            produce(t, 1 - place["core"], send_core.at[t % CORE_SLOTS])
            if t >= CORE_SLOTS:
                pl.semaphore_wait(core_free, 1)
            core_copy(t).start()
            produce(t, place["core"], sums.at[t % SUM_SLOTS])
            if fetched(t + 2):
                fetch(t + 2).start()
        for stage in (0, 1):
            old = t - LAG[stage]
            if 0 <= old < count:
                stage_add(old, stage)
                stage_start(old, stage + 1)
        old = t - LAG[2]
        if 0 <= old < count:
            here = stage_add(old, 2)
            kind, _, _, _, out, column = chunks[old]
            total = sums[old % SUM_SLOTS, here]
            if kind == "down":
                out[:, pl.ds(column, WIDE)] = total
            else:
                high = out.shape[0]
                for part in range(width // WIDE):
                    out[:, pl.ds(column + part * WIDE, WIDE)] = total[part * high : (part + 1) * high]
        if t < len(small_axes):
            for one in small_copies(t):
                one.wait()
            value = small_out[...]
            for offset in range(1, size[small_axes[t]]):
                value = value + small_recv[t, offset - 1]
            small_out[...] = value
            if t + 1 < len(small_axes):
                for one in small_copies(t + 1):
                    one.start()
    for t in range(count - CORE_SLOTS, count):
        core_copy(t).wait_send()


def reduce_weights(act, second, mixed, first, grad, d_pre, d_query, d_key, d_value, small):
    rows, width = grad.shape
    size = sizes()
    devices = size["y"] * 2 * size["far"] * size["near"]
    units = devices // 2
    unit = (act.shape[1] // devices, WIDE)
    most = max(size["y"], size["near"]) - 1
    fewest = min(size["y"], size["near"])
    first_part = most * units // (most + 1) if most + 1 == fewest else most * units // fewest
    dma = pltpu.SemaphoreType.DMA
    free = pltpu.SemaphoreType.REGULAR
    stage_sems = []
    for peers in (most, most, size["far"] - 1):
        stage_sems += [dma((STAGE_SLOTS, peers)), dma((STAGE_SLOTS, peers))]
    down_rows, side = act.shape[1] // devices, width // devices
    return pl.pallas_call(
        reduce_kernel,
        in_specs=[VMEM] * 5 + [ANY] * 4 + [VMEM],
        out_specs=[VMEM] * 5,
        out_shape=[
            jax.ShapeDtypeStruct((down_rows, width), F32),
            jax.ShapeDtypeStruct((side, d_pre.shape[1]), F32),
            jax.ShapeDtypeStruct((side, width), F32),
            jax.ShapeDtypeStruct((side, 3 * width), F32),
            jax.ShapeDtypeStruct(small.shape, F32),
        ],
        scratch_shapes=[
            pltpu.VMEM((2, rows, width), BF16),
            pltpu.VMEM((CORE_SLOTS, units, *unit), F32),
            pltpu.VMEM((CORE_SLOTS, units, *unit), F32),
            pltpu.VMEM((SUM_SLOTS, units, *unit), F32),
            pltpu.VMEM((STAGE_SLOTS, first_part, *unit), F32),
            pltpu.VMEM((STAGE_SLOTS, max(1, first_part // fewest), *unit), F32),
            pltpu.VMEM((STAGE_SLOTS, size["far"] - 1, *unit), F32),
            pltpu.VMEM((4, max(most, size["far"] - 1), *small.shape), F32),
            dma((2,)), dma((CORE_SLOTS,)), dma((CORE_SLOTS,)),
            *stage_sems,
            dma((4, max(most, size["far"] - 1))), dma((4, max(most, size["far"] - 1))),
            free, free((2, most)), free((2, most)), free((2, size["far"] - 1)),
        ],
        compiler_params=pltpu.CompilerParams(
            collective_id=3, has_side_effects=True, vmem_limit_bytes=LIMIT
        ),
        name="reduce_weights",
    )(act, second, mixed, first, grad, d_pre, d_query, d_key, d_value, small)


def exchange_kernel(
    state, stat, before, after, from_low, from_high, to_high, to_low, near_low, near_high,
    up_send, up_got, down_send, down_got, low_send, low_got, high_send, high_got,
):
    size, place = sizes(), places()
    far, near = place["far"], place["near"]
    slots = state.shape[0]
    greet(("far", "near"))

    def hop(source, target, send, recv, axis, offset):
        return pltpu.make_async_remote_copy(
            src_ref=source, dst_ref=target, send_sem=send, recv_sem=recv,
            device_id=peer(axis, offset), device_id_type=MESH,
        )

    up = lambda i: hop(to_high.at[i], from_low.at[i], up_send.at[i], up_got.at[i], "far", 1)
    down = lambda i: hop(
        to_low.at[i], from_high.at[i], down_send.at[i], down_got.at[i], "far", size["far"] - 1
    )

    def beside(i, offset, source, target, send, got):
        return hop(
            source.at[i], target.at[offset - 1, i], send.at[offset - 1, i], got.at[offset - 1, i],
            "near", offset,
        )

    def forward(i):
        @pl.when(far == 0)
        def _():
            from_low[i] = jnp.zeros(state.shape[1:], F32)

        @pl.when(far > 0)
        def _():
            up(i).wait_recv()

        to_high[i] = from_low[i] + state[i]

        @pl.when(far < size["far"] - 1)
        def _():
            up(i).start()

        for offset in range(1, size["near"]):
            later = near + offset < size["near"]

            @pl.when(later)
            def _():
                beside(i, offset, to_high, near_low, low_send, low_got).start()

            @pl.when(jnp.logical_not(later))
            def _():
                beside(i, offset, from_low, near_low, low_send, low_got).start()

    def backward(i):
        @pl.when(far == size["far"] - 1)
        def _():
            from_high[i] = jnp.zeros(state.shape[1:], F32)

        @pl.when(far < size["far"] - 1)
        def _():
            down(i).wait_recv()

        to_low[i] = from_high[i] + stat[i]

        @pl.when(far > 0)
        def _():
            down(i).start()

        for offset in range(1, size["near"]):
            later = near + offset < size["near"]

            @pl.when(later)
            def _():
                beside(i, offset, from_high, near_high, high_send, high_got).start()

            @pl.when(jnp.logical_not(later))
            def _():
                beside(i, offset, to_low, near_high, high_send, high_got).start()

    for i in range(slots):
        forward(i)
        backward(i)
    for i in range(slots):
        low, high = from_low[i], from_high[i]
        for offset in range(1, size["near"]):
            beside(i, offset, to_high, near_low, low_send, low_got).wait_recv()
            beside(i, offset, to_low, near_high, high_send, high_got).wait_recv()
            low = low + near_low[offset - 1, i]
            high = high + near_high[offset - 1, i]
        before[i] = low
        after[i] = high
    for i in range(slots):
        @pl.when(far < size["far"] - 1)
        def _():
            up(i).wait_send()

        @pl.when(far > 0)
        def _():
            down(i).wait_send()

        for offset in range(1, size["near"]):
            beside(i, offset, to_high, near_low, low_send, low_got).wait_send()
            beside(i, offset, to_low, near_high, high_send, high_got).wait_send()


def exchange(state, stat):
    slots = state.shape[0]
    beside = sizes()["near"] - 1
    dma = pltpu.SemaphoreType.DMA
    shape = jax.ShapeDtypeStruct(state.shape, F32)
    return pl.pallas_call(
        exchange_kernel,
        in_specs=[VMEM] * 2,
        out_specs=[VMEM] * 2,
        out_shape=[shape, shape],
        scratch_shapes=[pltpu.VMEM(state.shape, F32)] * 4
        + [pltpu.VMEM((beside, *state.shape), F32)] * 2
        + [dma((slots,))] * 4
        + [dma((beside, slots))] * 4,
        compiler_params=pltpu.CompilerParams(
            collective_id=4, has_side_effects=True, vmem_limit_bytes=LIMIT
        ),
        name="exchange",
    )(state, stat)


def diagonal_blocks(small, copies):
    return jnp.kron(jnp.eye(copies, dtype=F32), small)


def per_device(
    hidden_in, cotangent, lengths, ln1_gain, ln1_bias, ln2_gain, ln2_bias, qkv_weight, qkv_bias,
    dense_weight, dense_bias, up_weight, up_bias, down_weight, down_bias, feature_gain, projection,
):
    slots, toks, width = hidden_in.shape
    heads, feats = feature_gain.shape
    head = width // heads
    rows = slots * toks
    half = ROT // 2
    hidden = hidden_in.reshape(rows, width)
    grad = cotangent.reshape(rows, width)
    position = lax.axis_index("seq") * toks + jnp.arange(toks)
    live = (position[None, :] < lengths[:, None]).astype(F32).reshape(rows, 1)
    frequency = 10000.0 ** (-2.0 * jnp.arange(half).astype(F32) / ROT)
    angle = position.astype(F32)[:, None] * frequency[None, :]
    blank = jnp.zeros((toks, half), F32)
    rest = head - ROT
    cosine = jnp.concatenate([jnp.cos(angle), jnp.cos(angle), jnp.ones((toks, rest), F32)], 1)
    sine_a = jnp.concatenate([-jnp.sin(angle), blank, jnp.zeros((toks, rest), F32)], 1)
    sine_b = jnp.concatenate([blank, jnp.sin(angle), jnp.zeros((toks, rest), F32)], 1)
    tables = (cosine, sine_a, sine_b)
    wide_tables = tuple(jnp.tile(t, (TILE // toks, WIDE // head)) for t in tables)
    slot_tables = tuple(jnp.tile(t, (1, LANES // head)) for t in tables)
    tile_tables = tuple(jnp.tile(t, (TILE // toks, LANES // head)) for t in tables)
    dct = dct_matrix(head)
    feature_matrix = jnp.dot(dct.T, projection, precision=lax.Precision.HIGHEST)
    big = diagonal_blocks(feature_matrix, WIDE // head)
    maps = split(big)
    map_back = diagonal_blocks(feature_matrix.T, LANES // head).astype(BF16)
    row = lambda v: v.reshape(1, -1)
    first, second, query, key, value, query_rot, key_rot, state, total = front(
        hidden, qkv_weight, row(qkv_bias), row(ln1_gain), row(ln1_bias), row(ln2_gain), row(ln2_bias),
        wide_tables, maps, row(feature_gain), live, slots, head,
    )
    d_num, inverse, prior, stat, grad_sum = middle(grad, dense_weight, query, key, total, slots, head)
    before, after = exchange(state, stat)
    act, d_pre, branch, d_second, up_bias_grad = mlp(second, grad, up_weight, row(up_bias), down_weight)
    mixed, d_query, d_value, d_key_part, query_norm, gain_q, map_q, bias_qv = attend(
        query, key, value, query_rot, d_num, inverse, before, after, prior, slot_tables, map_back, slots, head
    )
    output, input_grad, d_key, norm_sums, gain_k, map_k, bias_k = back(
        (hidden, grad, mixed, branch, d_second, key, key_rot, d_key_part, d_query, d_value, query_norm,
         qkv_weight, dense_weight, row(dense_bias), row(down_bias), row(ln1_gain), row(ln2_gain)),
        tile_tables, map_back, slots, head,
    )
    small = jnp.concatenate(
        [norm_sums.reshape(-1), bias_qv[0, 0], bias_k[0], bias_qv[1, 0], grad_sum[0], up_bias_grad[0],
         (gain_q + gain_k)[0], (map_q + map_k).reshape(-1)]
    ).reshape(-1, LANES)
    down_grad, up_grad, dense_grad, qkv_grad, small = reduce_weights(
        act, second, mixed, first, grad, d_pre, d_query, d_key, d_value, small
    )
    small = small.reshape(-1)
    device = lax.axis_index("batch") * lax.axis_size("seq") + lax.axis_index("seq")
    devices = lax.axis_size("batch") * lax.axis_size("seq")
    start = 0
    vectors = []
    for length in (width, width, width, width, 2 * width, width, width, up_bias.shape[0]):
        share = length // devices
        vectors.append(lax.dynamic_slice(small, (start + device * share,), (share,)))
        start += length
    gain1_grad, shift1_grad, gain2_grad, shift2_grad, qk_grad, v_grad, g_sum, up_bias_share = vectors
    gain_grad = small[start : start + width].reshape(heads, feats) / feature_gain
    map_total = small[start + width :].reshape(LANES, LANES)
    map_total = map_total[:head, :head] + map_total[head:, head:]
    projection_grad = jnp.dot(dct, map_total, precision=lax.Precision.HIGHEST)
    return (
        output.reshape(hidden_in.shape), input_grad.reshape(hidden_in.shape),
        gain1_grad, shift1_grad, gain2_grad, shift2_grad,
        qkv_grad, qk_grad, v_grad, dense_grad, g_sum, up_grad, up_bias_share, down_grad, g_sum,
        gain_grad, projection_grad,
    )


def solution(mesh):
    rows = P("batch", "seq", None)
    both = P(("batch", "seq"))
    wide = P(("batch", "seq"), None)
    return jax.shard_map(
        per_device,
        mesh=mesh,
        in_specs=(rows, rows, P("batch")) + (P(),) * 14,
        out_specs=(rows, rows, both, both, both, both, wide, both, both, wide, both, wide, both, wide, both, P(), P()),
        check_vma=False,
    )
```
